256 devices in a mesh: cuts: 4 (over y_lo, core), shard: 64 (over z, x, y_hi).
Axes of the slice: x: 4, y: 4 (y_hi: 2, y_lo: 2; y = y_hi * 2 + y_lo), z: 8, core: 2. Of those that a mesh axis runs over, the one named last changes fastest.
Arguments:
- stems: float32 [4, 2, 16384, 8, 256], P('cuts', None, 'shard'), may hold values from -6 to 6
- slice_branches: float32 [6, 3, 2, 256, 256], replicated, may hold values from -0.25 to 0.25
- closing: float32 [2, 256, 256], replicated, may hold values from -0.25 to 0.25
- path: int32 [3], replicated, may hold values from 0 to 2, each once
- slice_assign: int32 [6], replicated, may hold values from 0 to 5, each once
Outputs:
- amplitudes: float32 [2, 16384, 8, 256], P(None, 'shard', 'cuts')
The draws below stay inside these ranges and needn't reach their ends.
Inputs may be any that keep to these rules, and one draw needn't show every extreme that they name: `path`: each value appears once. `slice_assign`: each value appears once.
All inputs are finite; a program needn't handle non-finite values.
Results may differ from the reference program's by a relative error of at most 0.00012.
Values sent between devices are 32-bit elements; how exact they have to be, the bound alone decides.
No kernel may reach another device: no remote copies, remote signals or barrier semaphores. Data moves between devices by JAX's collectives and lax.ppermute only.
A program may use at most 128 MiB of HBM per device.

```python
import jax
import jax.numpy as jnp
from jax import lax

BRANCH = 256
M = 8
NBR = 3
SLICE_VALUES = 6
SLOTS = 4
R = 16384
N_SHARD = 64


def levels(own_key, dims, pieces, smallest, top_value):
    factor_of, own = 1.0, jax.random.fold_in(own_key, 6)
    for position, shards_of in pieces:
        steps = jnp.exp(jax.random.uniform(jax.random.fold_in(own, position), (shards_of,), jnp.float32, smallest / len(pieces), top_value / len(pieces)))
        factor_of = factor_of * jnp.repeat(steps, dims[position] // shards_of).reshape([-1 if axis == position else 1 for axis in range(len(dims))])
    return factor_of


def gaussian(stream_key, shape, spread, most, shards=(), dtype=jnp.bfloat16):
    array = spread * jax.random.normal(stream_key, shape, jnp.float32)
    if shards:
        array = array * levels(stream_key, shape, shards, -0.22, 0.18)
    return jnp.clip(array, -most, most).astype(dtype)


def setup_inputs(seed: int = 0) -> dict:
    keys = jax.random.split(jax.random.key(seed), 6)
    return {
        "stems": gaussian(keys[0], (SLOTS, 2, R, M, BRANCH), 1.0, 6.0, ((0, 4), (2, 64)), jnp.float32),
        "slice_branches": gaussian(keys[1], (SLICE_VALUES, NBR, 2, BRANCH, BRANCH), (2 * BRANCH) ** -0.5, 0.25, (), jnp.float32),
        "closing": gaussian(keys[2], (2, BRANCH, BRANCH), (2 * BRANCH) ** -0.5, 0.25, (), jnp.float32),
        "path": jax.random.permutation(keys[3], NBR).astype(jnp.int32),
        "slice_assign": jax.random.permutation(keys[4], SLICE_VALUES).astype(jnp.int32),
    }


HIGH = lax.Precision.HIGHEST


def right_apply(field, matrix):
    prod = jnp.einsum('pglmk,qkn->pqglmn', field, matrix, precision=HIGH)
    return jnp.stack([prod[0, 0] - prod[1, 1], prod[0, 1] + prod[1, 0]])


def left_apply(field, matrix):
    prod = jnp.einsum('pglmk,qln->pqgnmk', field, matrix, precision=HIGH)
    return jnp.stack([prod[0, 0] - prod[1, 1], prod[0, 1] + prod[1, 0]])


def swap_inner(field):
    shape = field.shape
    split = field.reshape(2, N_SHARD, N_SHARD, BRANCH // N_SHARD, M, BRANCH)
    return jnp.transpose(split, (0, 2, 1, 3, 4, 5)).reshape(shape)


def swap_outer(field):
    shape = field.shape
    split = field.reshape(2, N_SHARD, BRANCH, M, N_SHARD, BRANCH // N_SHARD)
    return jnp.transpose(split, (0, 4, 2, 3, 1, 5)).reshape(shape)


def reference(stems, slice_branches, closing, path, slice_assign):
    def one_slot(total, index):
        field = lax.dynamic_index_in_dim(stems, index, 0, keepdims=False)
        field = field.reshape(2, N_SHARD, BRANCH, M, BRANCH)
        mine = lax.dynamic_index_in_dim(slice_branches, slice_assign[index], 0, keepdims=False)

        def branch_at(step):
            return lax.dynamic_index_in_dim(mine, path[step], 0, keepdims=False)

        field = left_apply(field, branch_at(0))
        field = right_apply(field, branch_at(1))
        field = swap_inner(field)
        field = left_apply(field, branch_at(2))
        field = swap_outer(field)
        return total + field, None

    start = jnp.zeros((2, N_SHARD, BRANCH, M, BRANCH), jnp.float32)
    total, unused = lax.scan(one_slot, start, jnp.arange(SLOTS).astype(jnp.int32))
    total = right_apply(total, closing)
    return total.reshape(2, R, M, BRANCH)
```

```python
import functools

import jax
import jax.numpy as jnp
from jax import lax
from jax.experimental import pallas as pl
from jax.experimental.pallas import tpu as pltpu
from jax.sharding import PartitionSpec as P

BF, F32 = jnp.bfloat16, jnp.float32
ALL = ("cuts", "shard")
NN = (((1,), (0,)), ((), ()))
NT = (((1,), (1,)), ((), ()))


def halves(x):
    high = x.astype(BF)
    return high, (x - high.astype(F32)).astype(BF)


def dot3(left, right, dims):
    dot = functools.partial(lax.dot_general, dimension_numbers=dims, preferred_element_type=F32)
    return dot(left[0], right[0]) + (dot(left[0], right[1]) + dot(left[1], right[0]))


def put(pair, rows, cols, value):
    high, low = halves(value)
    pair[0, rows, cols] = high
    pair[1, rows, cols] = low


def complex_blocks(pair, part, rows, cols, value):
    up = pl.ds(rows.start, rows.size), pl.ds(256 + rows.start, rows.size)
    across = pl.ds(cols.start, cols.size), pl.ds(256 + cols.start, cols.size)
    if part == 0:
        put(pair, up[0], across[0], value)
        put(pair, up[1], across[1], value)
    else:
        put(pair, up[1], across[0], value)
        put(pair, up[0], across[1], -value)


def before_kernel(assign, path, branches, x0, x1, send, v, tmp, a0, a1, sem):
    m = pl.program_id(0)

    @pl.when(m == 0)
    def _():
        value = assign[lax.axis_index("cuts")]
        copies = [pltpu.make_async_copy(branches.at[value, path[i]], v.at[i], sem.at[i]) for i in range(2)]
        for copy in copies:
            copy.start()
        for i, pair in enumerate((a0, a1)):
            copies[i].wait()
            for part in range(2):
                turned = v[i, part].T
                for half in range(2):
                    tmp[half] = turned[:, 128 * half : 128 * half + 128]
                for half in range(2):
                    for b in range(4):
                        value = tmp[half, pl.ds(b, 64, stride=4), :]
                        complex_blocks(pair, part, pl.ds(64 * b, 64), pl.ds(128 * half, 128), value)

    x = jnp.concatenate(
        [
            jnp.concatenate([x0[p, pl.ds(m, 256, stride=8), :], x1[p, pl.ds(m, 256, stride=8), :]], axis=1)
            for p in range(2)
        ],
        axis=0,
    )
    z = dot3((a0[0], a0[1]), halves(x), NN)
    z = jnp.concatenate([z[:256], z[256:]], axis=1)
    y = dot3((a1[0], a1[1]), halves(z), NT)
    low_lane = lax.broadcasted_iota(jnp.int32, (64, 128), 1) < 64
    for q in range(2):
        for bph in range(2):
            for bh in range(2):
                row = 256 * q + 128 * bph
                one = y[row : row + 64, 128 * bh : 128 * bh + 128]
                two = y[row + 64 : row + 128, 128 * bh : 128 * bh + 128]
                one_turned, two_turned = pltpu.roll(one, 64, 1), pltpu.roll(two, 64, 1)
                r = 16 * (m % 2) + ((q * 2 + bph) * 4 + bh * 2)
                send[pl.ds(r, 64, stride=32), :] = jnp.where(low_lane, one, two_turned)
                send[pl.ds(r + 1, 64, stride=32), :] = jnp.where(low_lane, one_turned, two)


def after_kernel(assign, path, branches, closing, got, out, v, c, tmp, a2, c2, total, sem):
    s = pl.program_id(0)

    def fetch(i):
        return pltpu.make_async_copy(branches.at[assign[i], path[2]], v.at[lax.rem(i, 2)], sem.at[lax.rem(i, 2)])

    @pl.when(s == 0)
    def _():
        fetch(0).start()
        pltpu.make_async_copy(closing, c, sem.at[2]).start()

    @pl.when(s < 3)
    def _():
        fetch(s + 1).start()

    fetch(s).wait()
    for part in range(2):
        for half in range(2):
            tmp[half] = v[lax.rem(s, 2), part, :, pl.ds(128 * half, 128)]
        for half in range(2):
            moved = jnp.concatenate([tmp[half, pl.ds(b, 64, stride=4), :] for b in range(4)], axis=0)
            complex_blocks(a2, part, pl.ds(128 * half, 128), pl.ds(0, 256), moved.T)

    def rows_of(mj, p, bph):
        return jnp.concatenate(
            [got[pl.ds(((mj * 2 + p) * 2 + bph) * 4 + b, 64, stride=32), :] for b in range(4)], axis=0
        )

    for mj in range(2):
        right = jnp.concatenate(
            [jnp.concatenate([rows_of(mj, p, 0), rows_of(mj, p, 1)], axis=1) for p in range(2)], axis=0
        )
        product = dot3((a2[0], a2[1]), halves(right), NN)

        @pl.when(s == 0)
        def _():
            total[mj] = product

        @pl.when(s > 0)
        def _():
            total[mj] += product

    @pl.when(s == 3)
    def _():
        pltpu.make_async_copy(closing, c, sem.at[2]).wait()
        for part in range(2):
            for half in range(2):
                tmp[half] = c[part, :, pl.ds(128 * half, 128)]
            for half in range(2):
                for b in range(4):
                    value = tmp[half, pl.ds(b, 64, stride=4), :]
                    at = 64 * b, 128 * half
                    if part == 0:
                        put(c2, pl.ds(at[0], 64), pl.ds(at[1], 128), value)
                        put(c2, pl.ds(256 + at[0], 64), pl.ds(256 + at[1], 128), value)
                    else:
                        put(c2, pl.ds(at[0], 64), pl.ds(256 + at[1], 128), value)
                        put(c2, pl.ds(256 + at[0], 64), pl.ds(at[1], 128), -value)
        for mj in range(2):
            left = jnp.concatenate([total[mj, :256], total[mj, 256:]], axis=1)
            result = dot3(halves(left), (c2[0], c2[1]), NN)
            for q in range(2):
                for half in range(2):
                    cols = 256 * q + 128 * half
                    out[pl.ds(1024 * q + 2 * half + mj, 256, stride=4), :] = result[:, cols : cols + 128]


SMEM = pl.BlockSpec(memory_space=pltpu.SMEM)
ANY = pl.BlockSpec(memory_space=pl.ANY)
PARAMS = pltpu.CompilerParams(vmem_limit_bytes=48 * 2**20)


def per_device(stems, slice_branches, closing, path, slice_assign):
    x = stems.reshape(2, 2048, 256)
    send = pl.pallas_call(
        before_kernel,
        grid=(8,),
        in_specs=[
            SMEM,
            SMEM,
            ANY,
            pl.BlockSpec((2, 2048, 128), lambda m: (0, 0, 0)),
            pl.BlockSpec((2, 2048, 128), lambda m: (0, 0, 1)),
        ],
        out_specs=pl.BlockSpec((2048, 128), lambda m: (m // 2, 0)),
        out_shape=jax.ShapeDtypeStruct((8192, 128), F32),
        scratch_shapes=[
            pltpu.VMEM((2, 2, 256, 256), F32),
            pltpu.VMEM((2, 256, 128), F32),
            pltpu.VMEM((2, 512, 512), BF),
            pltpu.VMEM((2, 512, 512), BF),
            pltpu.SemaphoreType.DMA((2,)),
        ],
        compiler_params=PARAMS,
        name="before",
    )(slice_assign, path, slice_branches, x, x)
    got = lax.all_to_all(send.reshape(256, 32, 128), ALL, 0, 0, tiled=True).reshape(8192, 128)
    out = pl.pallas_call(
        after_kernel,
        grid=(4,),
        in_specs=[SMEM, SMEM, ANY, ANY, pl.BlockSpec((2048, 128), lambda s: (s, 0))],
        out_specs=pl.BlockSpec((2048, 128), lambda s: (0, 0)),
        out_shape=jax.ShapeDtypeStruct((2048, 128), F32),
        scratch_shapes=[
            pltpu.VMEM((2, 2, 256, 256), F32),
            pltpu.VMEM((2, 256, 256), F32),
            pltpu.VMEM((2, 256, 128), F32),
            pltpu.VMEM((2, 512, 512), BF),
            pltpu.VMEM((2, 512, 512), BF),
            pltpu.VMEM((2, 512, 256), F32),
            pltpu.SemaphoreType.DMA((3,)),
        ],
        compiler_params=PARAMS,
        name="after",
    )(slice_assign, path, slice_branches, closing, got)
    out = out.reshape(2, 256, 2, 2, 128)
    return jnp.transpose(out, (0, 1, 3, 2, 4)).reshape(2, 256, 2, 256)


def solution(mesh):
    return jax.shard_map(
        per_device,
        mesh=mesh,
        in_specs=(P("cuts", None, "shard", None, None), P(), P(), P(), P()),
        out_specs=P(None, "shard", "cuts", None),
        check_vma=False,
    )
```

```python
import functools

import jax
import jax.numpy as jnp
from jax import lax
from jax.experimental import pallas as pl
from jax.experimental.pallas import tpu as pltpu
from jax.sharding import PartitionSpec as P

BF, F32 = jnp.bfloat16, jnp.float32
ALL = ("cuts", "shard")


def halves(x):
    high = x.astype(BF)
    return high, (x - high.astype(F32)).astype(BF)


def dot3(left, right):
    dot = functools.partial(jnp.dot, preferred_element_type=F32)
    rows = left.shape[0] // 2
    both = dot(left, right[0])
    return both[:rows] + (both[rows:] + dot(left[:rows], right[1]))


def stacked(x):
    return cat(halves(x), 0)


def put(pair, rows, cols, value):
    pair[0, rows, cols], pair[1, rows, cols] = halves(value)


def right_blocks(pair, part, value):
    one, two = slice(0, 256), slice(256, 512)
    if part == 0:
        put(pair, one, one, value)
        put(pair, two, two, value)
    else:
        put(pair, one, two, value)
        put(pair, two, one, -value)


def cat(pieces, axis):
    return jnp.concatenate(pieces, axis=axis)


def before_kernel(assign, path, branches, x, send, words, steps, xs, v, tmp, w1, w0, ys, word_sem, x_sem, v_sem, y_sem):
    words_in = [pltpu.make_async_copy(a, to, word_sem.at[i]) for i, (a, to) in enumerate(((assign, words), (path, steps)))]
    stem = [
        pltpu.make_async_copy(x.at[p, :, pl.ds(128 * h, 128)], xs.at[p, h], x_sem.at[p, h])
        for p in range(2)
        for h in range(2)
    ]
    for copy in words_in:
        copy.start()
    for copy in stem:
        copy.start()
    for copy in words_in:
        copy.wait()
    value = words[lax.axis_index("cuts")]
    weights = [pltpu.make_async_copy(branches.at[value, steps[i]], v.at[i], v_sem.at[i]) for i in (1, 0)]
    for copy in weights:
        copy.start()
    for copy, pair, index in zip(weights, (w1, w0), (1, 0), strict=True):
        copy.wait()
        for part in range(2):
            turned = v[index, part].T
            for h in range(2):
                tmp[h] = turned[:, 128 * h : 128 * h + 128]
            moved = [cat([tmp[h, pl.ds(b, 64, stride=4), :] for b in range(4)], 0) for h in range(2)]
            right_blocks(pair, part, cat(moved, 1).T)
    for copy in stem:
        copy.wait()
    low_lane = lax.broadcasted_iota(jnp.int32, (64, 128), 1) < 64

    def along_k(m):
        field = cat([xs[p, h, pl.ds(m, 256, stride=8), :] for p in range(2) for h in range(2)], 1)
        return dot3(stacked(field), (w1[0], w1[1]))

    later = along_k(0)
    for m in range(8):
        c, parity = m // 2, m % 2
        z = later
        if PIPELINED and m < 7:
            later = along_k(m + 1)
        z = cat([z[:, :256].T, z[:, 256:].T], 1)
        y = dot3(stacked(z), (w0[0], w0[1]))
        if not PIPELINED and m < 7:
            later = along_k(m + 1)
        for q in range(2):
            for bph in range(2):
                for bh in range(2):
                    cols = slice(256 * q + 128 * bh, 256 * q + 128 * bh + 128)
                    one = y[128 * bph : 128 * bph + 64, cols]
                    two = y[128 * bph + 64 : 128 * bph + 128, cols]
                    r = 2048 * c + 16 * parity + (q * 2 + bph) * 4 + bh * 2
                    ys[pl.ds(r, 64, stride=32), :] = jnp.where(low_lane, one, pltpu.roll(two, 64, 1))
                    ys[pl.ds(r + 1, 64, stride=32), :] = jnp.where(low_lane, pltpu.roll(one, 64, 1), two)
        if parity == 1:
            rows = pl.ds(2048 * c, 2048)
            pltpu.make_async_copy(ys.at[rows], send.at[rows], y_sem.at[c]).start()
    for c in range(4):
        rows = pl.ds(2048 * c, 2048)
        pltpu.make_async_copy(ys.at[rows], send.at[rows], y_sem.at[c]).wait()


def matrices_kernel(assign, path, branches, closing, a2, c2, v, c, tmp, v_sem, c_sem):
    copies = [
        pltpu.make_async_copy(
            branches.at[assign[s], path[2], p, :, pl.ds(128 * h, 128)], v.at[s, p, h], v_sem.at[s, p, h]
        )
        for s in range(4)
        for p in range(2)
        for h in range(2)
    ]
    last = pltpu.make_async_copy(closing, c, c_sem)
    for copy in copies:
        copy.start()
    last.start()
    for copy in copies:
        copy.wait()
    for s in range(4):
        for p in range(2):
            moved = [cat([v[s, p, h, pl.ds(b, 64, stride=4), :] for b in range(4)], 0) for h in range(2)]
            piece = cat(moved, 1).T
            one, two = slice(512 * s, 512 * s + 256), slice(512 * s + 256, 512 * s + 512)
            for at, cols, value in (
                ((0, one, piece), (256, two, piece)) if p == 0 else ((256, one, piece), (0, two, -piece))
            ):
                a2[at : at + 256, cols], a2[512 + at : 768 + at, cols] = halves(value)
    last.wait()
    for p in range(2):
        for h in range(2):
            tmp[h] = c[p, :, 128 * h : 128 * h + 128]
        moved = cat([cat([tmp[h, pl.ds(b, 64, stride=4), :] for b in range(4)], 0) for h in range(2)], 1)
        right_blocks(c2, p, moved)


def after_kernel(got, a2, c2, out, rs, a2s, r_sem, a_sem):
    def reads(s):
        rows = pl.ds(2048 * s, 2048)
        return (
            pltpu.make_async_copy(a2.at[:, pl.ds(512 * s, 512)], a2s.at[s], a_sem.at[s]),
            pltpu.make_async_copy(got.at[rows], rs.at[rows], r_sem.at[s]),
        )

    for s in range(4):
        for copy in reads(s):
            copy.start()
    total = None
    for s in range(4):
        for copy in reads(s):
            copy.wait()

        def sources(parity, p, bph):
            at = 2048 * s + 16 * parity + (p * 2 + bph) * 4
            return cat([rs[pl.ds(at + b, 64, stride=32), :] for b in range(4)], 0)

        right = cat(
            [cat([sources(parity, p, bph) for parity in range(2) for bph in range(2)], 1) for p in range(2)], 0
        )
        term = dot3(a2s[s], halves(right))
        total = term if total is None else total + term
    left = cat([cat([total[:256, cols], total[256:, cols]], 1) for cols in (slice(0, 256), slice(256, 512))], 0)
    result = dot3(stacked(left), (c2[0], c2[1]))
    for parity in range(2):
        for q in range(2):
            for h in range(2):
                cols = slice(256 * q + 128 * h, 256 * q + 128 * h + 128)
                out[pl.ds(1024 * q + 2 * h + parity, 256, stride=4), :] = result[256 * parity : 256 * parity + 256, cols]


PIPELINED = True
SMEM = pl.BlockSpec(memory_space=pltpu.SMEM)
HBM = pl.BlockSpec(memory_space=pltpu.HBM)
VMEM = pl.BlockSpec(memory_space=pltpu.VMEM)
DMA = pltpu.SemaphoreType.DMA


def kernel_call(kernel, in_specs, out_specs, shapes, operands, name, scratch, mib):
    return pl.pallas_call(
        kernel,
        in_specs=in_specs,
        out_specs=out_specs,
        out_shape=shapes,
        scratch_shapes=scratch,
        compiler_params=pltpu.CompilerParams(vmem_limit_bytes=mib * 2**20),
        name=name,
    )(*operands)


def shaped(*shape, dtype=F32):
    return jax.ShapeDtypeStruct(shape, dtype)


def before(operands):
    return kernel_call(
        before_kernel,
        [HBM] * 4,
        [HBM],
        [pltpu.HBM((8192, 128), F32)],
        operands,
        "before",
        [
            pltpu.SMEM((6,), jnp.int32),
            pltpu.SMEM((3,), jnp.int32),
            pltpu.VMEM((2, 2, 2048, 128), F32),
            pltpu.VMEM((2, 2, 256, 256), F32),
            pltpu.VMEM((2, 256, 128), F32),
            pltpu.VMEM((2, 512, 512), BF),
            pltpu.VMEM((2, 512, 512), BF),
            pltpu.VMEM((8192, 128), F32),
            DMA((2,)),
            DMA((2, 2)),
            DMA((2,)),
            DMA((4,)),
        ],
        32,
    )[0]


def matrices(operands):
    return kernel_call(
        matrices_kernel,
        [SMEM, SMEM, HBM, HBM],
        [VMEM, VMEM],
        [pltpu.HBM((1024, 2048), BF), shaped(2, 512, 512, dtype=BF)],
        operands,
        "matrices",
        [
            pltpu.VMEM((4, 2, 2, 256, 128), F32),
            pltpu.VMEM((2, 256, 256), F32),
            pltpu.VMEM((2, 256, 128), F32),
            DMA((4, 2, 2)),
            DMA,
        ],
        24,
    )


def after(got, a2, c2):
    return kernel_call(
        after_kernel,
        [HBM, HBM, VMEM],
        [VMEM],
        [shaped(2048, 128)],
        (got, a2, c2),
        "after",
        [pltpu.VMEM((8192, 128), F32), pltpu.VMEM((4, 1024, 512), BF), DMA((4,)), DMA((4,))],
        32,
    )[0]


def in_hbm(a):
    return pltpu.with_memory_space_constraint(a, pltpu.HBM)


def per_device(stems, slice_branches, closing, path, slice_assign):
    branches = in_hbm(slice_branches)
    send = before((in_hbm(slice_assign), in_hbm(path), branches, in_hbm(stems.reshape(2, 2048, 256))))
    a2, c2 = matrices((slice_assign, path, branches, in_hbm(closing)))
    got = lax.all_to_all(send.reshape(256, 32, 128), ALL, 0, 0, tiled=True).reshape(8192, 128)
    out = after(in_hbm(got), in_hbm(a2), c2)
    out = out.reshape(2, 256, 2, 2, 128)
    return jnp.transpose(out, (0, 1, 3, 2, 4)).reshape(2, 256, 2, 256)


def solution(mesh):
    return jax.shard_map(
        per_device,
        mesh=mesh,
        in_specs=(P("cuts", None, "shard", None, None), P(), P(), P(), P()),
        out_specs=P(None, "shard", "cuts", None),
        check_vma=False,
    )
```

```python
import functools

import jax
import jax.numpy as jnp
from jax import lax
from jax.experimental import pallas as pl
from jax.experimental.pallas import tpu as pltpu
from jax.sharding import PartitionSpec as P

BF, F32 = jnp.bfloat16, jnp.float32
ALL = ("cuts", "shard")


def halves(x):
    high = x.astype(BF)
    return high, (x - high.astype(F32)).astype(BF)


def dot3(left, right):
    dot = functools.partial(jnp.dot, preferred_element_type=F32)
    rows = left.shape[0] // 2
    both = dot(left, right[0])
    return both[:rows] + (both[rows:] + dot(left[:rows], right[1]))


def stacked(x):
    return cat(halves(x), 0)


def put(pair, rows, cols, value):
    pair[0, rows, cols], pair[1, rows, cols] = halves(value)


def right_blocks(pair, part, value):
    one, two = slice(0, 256), slice(256, 512)
    if part == 0:
        put(pair, one, one, value)
        put(pair, two, two, value)
    else:
        put(pair, one, two, value)
        put(pair, two, one, -value)


def cat(pieces, axis):
    return jnp.concatenate(pieces, axis=axis)


def before_kernel(assign, path, branches, x, send, words, steps, xs, v, tmp, mix, w1, w0, ys, word_sem, x_sem, v_sem, y_sem):
    words_in = [pltpu.make_async_copy(a, to, word_sem.at[i]) for i, (a, to) in enumerate(((assign, words), (path, steps)))]
    stem = [
        pltpu.make_async_copy(x.at[p, :, pl.ds(128 * h, 128)], xs.at[p, h], x_sem.at[p, h])
        for p in range(2)
        for h in range(2)
    ]
    for copy in words_in:
        copy.start()
    for copy in stem:
        copy.start()
    for copy in words_in:
        copy.wait()
    value = words[lax.axis_index("cuts")]
    turn_by = lax.rem(lax.axis_index("shard"), 8)
    weights = [pltpu.make_async_copy(branches.at[value, steps[i]], v.at[i], v_sem.at[i]) for i in range(2)]
    for copy in (weights[1], weights[0]):
        copy.start()

    def turn(index, part):
        turned = v[index, part].T
        for h in range(2):
            tmp[h] = turned[:, 128 * h : 128 * h + 128]

    weights[1].wait()
    for part in range(2):
        turn(1, part)
        for h in range(2):
            for b in range(4):
                value = tmp[h, pl.ds(b, 64, stride=4), :]
                mix[h, pl.ds(lax.rem(b + 4 * part + turn_by, 8), 64, stride=8), :] = value
                mix[2 + h, pl.ds(lax.rem(b + 4 * (1 - part) + turn_by, 8), 64, stride=8), :] = -value if part else value
    for h in range(4):
        put(w1, slice(128 * h, 128 * h + 128), slice(0, 512), mix[h].T)

    for copy in stem:
        copy.wait()

    def along_k(m):
        field = cat([xs[p, h, pl.ds(m, 256, stride=8), :] for p in range(2) for h in range(2)], 1)
        return dot3(stacked(field), (w1[0], w1[1]))

    later = along_k(0)
    weights[0].wait()
    for part in range(2):
        turn(0, part)
        moved = [cat([tmp[h, pl.ds(b, 64, stride=4), :] for b in range(4)], 0) for h in range(2)]
        put(w0, slice(0, 256), slice(256 * part, 256 * part + 256), cat(moved, 1).T)
    imaginary = lax.rem(lax.broadcasted_iota(jnp.int32, (64, 8, 256), 1) + (8 - turn_by), 8) >= 4
    for m in range(8):
        c, parity = m // 2, m % 2
        z = later
        if m < 7:
            later = along_k(m + 1)
        u = dot3(stacked(z.T), (w0[0], w0[1])).reshape(64, 8, 512)
        across = pltpu.roll(u[:, :, 256:], 4, 1)
        y = u[:, :, :256] + jnp.where(imaginary, across, -across)
        for bh in range(2):
            r = 16 * parity + 8 * bh
            ys[64 * c : 64 * c + 64, r : r + 8, :] = y[:, :, 128 * bh : 128 * bh + 128]
        if parity == 1:
            rows = pl.ds(64 * c, 64)
            pltpu.make_async_copy(ys.at[rows], send.at[rows], y_sem.at[c]).start()
    for c in range(4):
        rows = pl.ds(64 * c, 64)
        pltpu.make_async_copy(ys.at[rows], send.at[rows], y_sem.at[c]).wait()


def matrices_kernel(assign, path, branches, closing, a2, c2, v, c, tmp, v_sem, c_sem):
    copies = [
        pltpu.make_async_copy(
            branches.at[assign[s], path[2], p, :, pl.ds(128 * h, 128)], v.at[s, p, h], v_sem.at[s, p, h]
        )
        for s in range(4)
        for p in range(2)
        for h in range(2)
    ]
    last = pltpu.make_async_copy(closing, c, c_sem)
    for copy in copies:
        copy.start()
    last.start()
    for copy in copies:
        copy.wait()
    for s in range(4):
        for p in range(2):
            moved = [cat([v[s, p, h, pl.ds(b, 64, stride=4), :] for b in range(4)], 0) for h in range(2)]
            at = 256 * p
            a2[s, at : at + 256, :], a2[s, 512 + at : 768 + at, :] = halves(cat(moved, 1).T)
    last.wait()
    for p in range(2):
        for h in range(2):
            tmp[h] = c[p, :, 128 * h : 128 * h + 128]
        moved = cat([cat([tmp[h, pl.ds(b, 64, stride=4), :] for b in range(4)], 0) for h in range(2)], 1)
        right_blocks(c2, p, moved)


def after_kernel(got, a2, c2, out, rs, r_sem):
    def read(s):
        rows = pl.ds(2048 * s, 2048)
        return pltpu.make_async_copy(got.at[rows], rs.at[s, pl.ds(8, 2048)], r_sem.at[s])

    w = lax.broadcasted_iota(jnp.int32, (8, 128), 0)

    def row_of(s, block, j):
        rows = []
        for z in range(8):
            at = 256 * z + 8 * block + j + 8
            straight = rs[s, pl.ds(at, 8, stride=33), :]
            rows.append(jnp.where(w + j < 8, straight, rs[s, pl.ds(at - 8, 8, stride=33), :]) if j else straight)
        return cat(rows, 0)

    low_lane = lax.broadcasted_iota(jnp.int32, (64, 128), 1) < 64

    def sources(s, p, parity, bph):
        rows = []
        for bh in range(2):
            one, two = (row_of(s, 2 * parity + bh, 4 * p + 2 * bph + bpl) for bpl in range(2))
            crossed = pltpu.roll(jnp.where(low_lane, two, one), 64, 1)
            rows += [jnp.where(low_lane, one, crossed), jnp.where(low_lane, crossed, two)]
        return cat(rows, 0)

    def arrived(s):
        read(s).wait()
        return halves(cat([sources(s, p, m, bph) for p in range(2) for m in range(2) for bph in range(2)], 1))

    for s in range(4):
        read(s).start()
        rs[s, 0:8] = rs[s, 2056:2064] = jnp.zeros((8, 128), F32)
    later, total = arrived(0), None
    for s in range(4):
        right = later
        if s < 3:
            later = arrived(s + 1)
        term = dot3(a2[s], right)
        total = term if total is None else total + term
    real = total[:256, :512] - total[256:, 512:]
    imaginary = total[256:, :512] + total[:256, 512:]
    left = cat([cat([real[:, cols], imaginary[:, cols]], 1) for cols in (slice(0, 256), slice(256, 512))], 0)
    result = dot3(stacked(left), (c2[0], c2[1]))
    for parity in range(2):
        for q in range(2):
            for h in range(2):
                cols = slice(256 * q + 128 * h, 256 * q + 128 * h + 128)
                out[pl.ds(1024 * q + 2 * h + parity, 256, stride=4), :] = result[256 * parity : 256 * parity + 256, cols]


SMEM = pl.BlockSpec(memory_space=pltpu.SMEM)
HBM = pl.BlockSpec(memory_space=pltpu.HBM)
VMEM = pl.BlockSpec(memory_space=pltpu.VMEM)
DMA = pltpu.SemaphoreType.DMA


def kernel_call(kernel, in_specs, out_specs, shapes, operands, name, scratch, mib):
    return pl.pallas_call(
        kernel,
        in_specs=in_specs,
        out_specs=out_specs,
        out_shape=shapes,
        scratch_shapes=scratch,
        compiler_params=pltpu.CompilerParams(vmem_limit_bytes=mib * 2**20),
        name=name,
    )(*operands)


def shaped(*shape, dtype=F32):
    return jax.ShapeDtypeStruct(shape, dtype)


def before(operands):
    return kernel_call(
        before_kernel,
        [HBM] * 4,
        [HBM],
        [pltpu.HBM((256, 32, 128), F32)],
        operands,
        "before",
        [
            pltpu.SMEM((6,), jnp.int32),
            pltpu.SMEM((3,), jnp.int32),
            pltpu.VMEM((2, 2, 2048, 128), F32),
            pltpu.VMEM((2, 2, 256, 256), F32),
            pltpu.VMEM((2, 256, 128), F32),
            pltpu.VMEM((4, 512, 128), F32),
            pltpu.VMEM((2, 512, 512), BF),
            pltpu.VMEM((2, 256, 512), BF),
            pltpu.VMEM((256, 32, 128), F32),
            DMA((2,)),
            DMA((2, 2)),
            DMA((2,)),
            DMA((4,)),
        ],
        32,
    )[0]


def matrices(operands):
    return kernel_call(
        matrices_kernel,
        [SMEM, SMEM, HBM, HBM],
        [VMEM, VMEM],
        [shaped(4, 1024, 256, dtype=BF), shaped(2, 512, 512, dtype=BF)],
        operands,
        "matrices",
        [
            pltpu.VMEM((4, 2, 2, 256, 128), F32),
            pltpu.VMEM((2, 256, 256), F32),
            pltpu.VMEM((2, 256, 128), F32),
            DMA((4, 2, 2)),
            DMA,
        ],
        24,
    )


def after(got, a2, c2):
    return kernel_call(
        after_kernel,
        [HBM, VMEM, VMEM],
        [VMEM],
        [shaped(2048, 128)],
        (got, a2, c2),
        "after",
        [pltpu.VMEM((4, 2064, 128), F32), DMA((4,))],
        28,
    )[0]


def in_hbm(a):
    return pltpu.with_memory_space_constraint(a, pltpu.HBM)


def per_device(stems, slice_branches, closing, path, slice_assign):
    branches = in_hbm(slice_branches)
    send = before((in_hbm(slice_assign), in_hbm(path), branches, in_hbm(stems.reshape(2, 2048, 256))))
    a2, c2 = matrices((slice_assign, path, branches, in_hbm(closing)))
    got = lax.all_to_all(send, ALL, 0, 0, tiled=True).reshape(8192, 128)
    out = after(in_hbm(got), a2, c2)
    out = out.reshape(2, 256, 2, 2, 128)
    return jnp.transpose(out, (0, 1, 3, 2, 4)).reshape(2, 256, 2, 256)


def solution(mesh):
    return jax.shard_map(
        per_device,
        mesh=mesh,
        in_specs=(P("cuts", None, "shard", None, None), P(), P(), P(), P()),
        out_specs=P(None, "shard", "cuts", None),
        check_vma=False,
    )
```

```python
import functools

import jax
import jax.numpy as jnp
from jax import lax
from jax.experimental import pallas as pl
from jax.experimental.pallas import tpu as pltpu
from jax.sharding import PartitionSpec as P

BF, F32 = jnp.bfloat16, jnp.float32
ALL = ("cuts", "shard")


def halves(x):
    high = x.astype(BF)
    return high, (x - high.astype(F32)).astype(BF)


def dot3(left, right):
    dot = functools.partial(jnp.dot, preferred_element_type=F32)
    rows = left.shape[0] // 2
    both = dot(left, right[0])
    return both[:rows] + (both[rows:] + dot(left[:rows], right[1]))


def stacked(x):
    return cat(halves(x), 0)


def put(pair, rows, cols, value):
    pair[0, rows, cols], pair[1, rows, cols] = halves(value)


def right_blocks(pair, part, value):
    one, two = slice(0, 256), slice(256, 512)
    if part == 0:
        put(pair, one, one, value)
        put(pair, two, two, value)
    else:
        put(pair, one, two, value)
        put(pair, two, one, -value)


def cat(pieces, axis):
    return jnp.concatenate(pieces, axis=axis)


def before_kernel(assign, path, branches, x, send, words, steps, xs, v, tmp, mix, w1, w0, ys, word_sem, x_sem, v_sem, y_sem):
    words_in = [pltpu.make_async_copy(a, to, word_sem.at[i]) for i, (a, to) in enumerate(((assign, words), (path, steps)))]
    stem = [
        pltpu.make_async_copy(x.at[p, :, pl.ds(128 * h, 128)], xs.at[p, h], x_sem.at[p, h])
        for p in range(2)
        for h in range(2)
    ]
    for copy in words_in:
        copy.start()
    for copy in stem:
        copy.start()
    for copy in words_in:
        copy.wait()
    value = words[lax.axis_index("cuts")]
    turn_by = lax.rem(lax.axis_index("shard"), 8)
    weights = [pltpu.make_async_copy(branches.at[value, steps[i]], v.at[i], v_sem.at[i]) for i in range(2)]
    for copy in (weights[1], weights[0]):
        copy.start()

    def turn(index, part):
        turned = v[index, part].T
        for h in range(2):
            tmp[h] = turned[:, 128 * h : 128 * h + 128]

    weights[1].wait()
    for part in range(2):
        turn(1, part)
        for h in range(2):
            for b in range(4):
                value = tmp[h, pl.ds(b, 64, stride=4), :]
                mix[h, pl.ds(lax.rem(b + 4 * part + turn_by, 8), 64, stride=8), :] = value
                mix[2 + h, pl.ds(lax.rem(b + 4 * (1 - part) + turn_by, 8), 64, stride=8), :] = -value if part else value
    for h in range(4):
        put(w1, slice(128 * h, 128 * h + 128), slice(0, 512), mix[h].T)

    for copy in stem:
        copy.wait()

    def along_k(m):
        field = cat([xs[p, h, pl.ds(m, 256, stride=8), :] for p in range(2) for h in range(2)], 1)
        return dot3(stacked(field), (w1[0], w1[1]))

    def write(m):
        where = pl.ds(64 * (m // 2), 64), pl.ds(16 * (m % 2), 16)
        return pltpu.make_async_copy(ys.at[where], send.at[where], y_sem.at[m])

    later = [along_k(0), along_k(1)]
    weights[0].wait()
    for part in range(2):
        turn(0, part)
        moved = [cat([tmp[h, pl.ds(b, 64, stride=4), :] for b in range(4)], 0) for h in range(2)]
        put(w0, slice(0, 256), slice(256 * part, 256 * part + 256), cat(moved, 1).T)
    imaginary = lax.rem(lax.broadcasted_iota(jnp.int32, (64, 8, 256), 1) + (8 - turn_by), 8) >= 4
    for m in range(8):
        c, parity = m // 2, m % 2
        z = later.pop(0)
        if m < 6:
            later.append(along_k(m + 2))
        u = dot3(stacked(z.T), (w0[0], w0[1])).reshape(64, 8, 512)
        across = pltpu.roll(u[:, :, 256:], 4, 1)
        y = u[:, :, :256] + jnp.where(imaginary, across, -across)
        for bh in range(2):
            r = 16 * parity + 8 * bh
            ys[64 * c : 64 * c + 64, r : r + 8, :] = y[:, :, 128 * bh : 128 * bh + 128]
        write(m).start()
    for m in range(8):
        write(m).wait()


def matrices_kernel(assign, path, branches, closing, a2, c2, v, c, tmp, v_sem, c_sem):
    copies = [
        pltpu.make_async_copy(
            branches.at[assign[s], path[2], p, :, pl.ds(128 * h, 128)], v.at[s, p, h], v_sem.at[s, p, h]
        )
        for s in range(4)
        for p in range(2)
        for h in range(2)
    ]
    last = pltpu.make_async_copy(closing, c, c_sem)
    for copy in copies:
        copy.start()
    last.start()
    for copy in copies:
        copy.wait()
    for s in range(4):
        for p in range(2):
            moved = [cat([v[s, p, h, pl.ds(b, 64, stride=4), :] for b in range(4)], 0) for h in range(2)]
            at = 256 * p
            a2[s, at : at + 256, :], a2[s, 512 + at : 768 + at, :] = halves(cat(moved, 1).T)
    last.wait()
    for p in range(2):
        for h in range(2):
            tmp[h] = c[p, :, 128 * h : 128 * h + 128]
        moved = cat([cat([tmp[h, pl.ds(b, 64, stride=4), :] for b in range(4)], 0) for h in range(2)], 1)
        right_blocks(c2, p, moved)


def after_kernel(got, a2, c2, out, rs, os, r_sem, o_sem):
    def read(s):
        rows = pl.ds(2048 * s, 2048)
        return pltpu.make_async_copy(got.at[rows], rs.at[s, pl.ds(8, 2048)], r_sem.at[s])

    w = lax.broadcasted_iota(jnp.int32, (8, 128), 0)

    def row_of(s, block, j):
        rows = []
        for z in range(8):
            at = 256 * z + 8 * block + j + 8
            straight = rs[s, pl.ds(at, 8, stride=33), :]
            rows.append(jnp.where(w + j < 8, straight, rs[s, pl.ds(at - 8, 8, stride=33), :]) if j else straight)
        return cat(rows, 0)

    low_lane = lax.broadcasted_iota(jnp.int32, (64, 128), 1) < 64

    def sources(s, p, parity, bph):
        rows = []
        for bh in range(2):
            one, two = (row_of(s, 2 * parity + bh, 4 * p + 2 * bph + bpl) for bpl in range(2))
            crossed = pltpu.roll(jnp.where(low_lane, two, one), 64, 1)
            rows += [jnp.where(low_lane, one, crossed), jnp.where(low_lane, crossed, two)]
        return cat(rows, 0)

    def arrived(s):
        read(s).wait()
        re, im = (cat([sources(s, p, m, bph) for m in range(2) for bph in range(2)], 1) for p in range(2))
        return halves(re), halves(re + im), halves(im - re)

    for s in range(4):
        read(s).start()
        rs[s, 0:8] = rs[s, 2056:2064] = jnp.zeros((8, 128), F32)
    later, total = arrived(0), None
    for s in range(4):
        right = later
        if s < 3:
            later = arrived(s + 1)
        parts = [a2[s, 256 * i : 256 * i + 256] for i in range(4)]
        both = parts[0].astype(F32) + parts[2].astype(F32) + (parts[1].astype(F32) + parts[3].astype(F32))
        lefts = stacked(both), cat(parts[1::2], 0), cat(parts[::2], 0)
        terms = [dot3(*pair) for pair in zip(lefts, right, strict=True)]
        total = terms if total is None else [a + b for a, b in zip(total, terms, strict=True)]
    real, imaginary = total[0] - total[1], total[0] + total[2]
    left = cat([cat([real[:, cols], imaginary[:, cols]], 1) for cols in (slice(0, 256), slice(256, 512))], 0)
    left = stacked(left)
    writes = []
    for q in range(2):
        result = dot3(left, (c2[0, :, 256 * q : 256 * q + 256], c2[1, :, 256 * q : 256 * q + 256]))
        for parity in range(2):
            for h in range(2):
                value = result[256 * parity : 256 * parity + 256, 128 * h : 128 * h + 128]
                os[pl.ds(1024 * q + 2 * h + parity, 256, stride=4), :] = value
        rows = pl.ds(1024 * q, 1024)
        writes.append(pltpu.make_async_copy(os.at[rows], out.at[rows], o_sem.at[q]))
        writes[q].start()
    for copy in writes:
        copy.wait()


SMEM = pl.BlockSpec(memory_space=pltpu.SMEM)
HBM = pl.BlockSpec(memory_space=pltpu.HBM)
VMEM = pl.BlockSpec(memory_space=pltpu.VMEM)
DMA = pltpu.SemaphoreType.DMA


def kernel_call(kernel, in_specs, out_specs, shapes, operands, name, scratch, mib):
    return pl.pallas_call(
        kernel,
        in_specs=in_specs,
        out_specs=out_specs,
        out_shape=shapes,
        scratch_shapes=scratch,
        compiler_params=pltpu.CompilerParams(vmem_limit_bytes=mib * 2**20),
        name=name,
    )(*operands)


def shaped(*shape, dtype=F32):
    return jax.ShapeDtypeStruct(shape, dtype)


def before(operands):
    return kernel_call(
        before_kernel,
        [HBM] * 4,
        [HBM],
        [pltpu.HBM((256, 32, 128), F32)],
        operands,
        "before",
        [
            pltpu.SMEM((6,), jnp.int32),
            pltpu.SMEM((3,), jnp.int32),
            pltpu.VMEM((2, 2, 2048, 128), F32),
            pltpu.VMEM((2, 2, 256, 256), F32),
            pltpu.VMEM((2, 256, 128), F32),
            pltpu.VMEM((4, 512, 128), F32),
            pltpu.VMEM((2, 512, 512), BF),
            pltpu.VMEM((2, 256, 512), BF),
            pltpu.VMEM((256, 32, 128), F32),
            DMA((2,)),
            DMA((2, 2)),
            DMA((2,)),
            DMA((8,)),
        ],
        32,
    )[0]


def matrices(operands):
    return kernel_call(
        matrices_kernel,
        [SMEM, SMEM, HBM, HBM],
        [VMEM, VMEM],
        [shaped(4, 1024, 256, dtype=BF), shaped(2, 512, 512, dtype=BF)],
        operands,
        "matrices",
        [
            pltpu.VMEM((4, 2, 2, 256, 128), F32),
            pltpu.VMEM((2, 256, 256), F32),
            pltpu.VMEM((2, 256, 128), F32),
            DMA((4, 2, 2)),
            DMA,
        ],
        24,
    )


def after(got, a2, c2):
    return kernel_call(
        after_kernel,
        [HBM, VMEM, VMEM],
        [HBM],
        [pltpu.HBM((2048, 128), F32)],
        (got, a2, c2),
        "after",
        [pltpu.VMEM((4, 2064, 128), F32), pltpu.VMEM((2048, 128), F32), DMA((4,)), DMA((2,))],
        28,
    )[0]


def in_hbm(a):
    return pltpu.with_memory_space_constraint(a, pltpu.HBM)


def per_device(stems, slice_branches, closing, path, slice_assign):
    branches = in_hbm(slice_branches)
    send = before((in_hbm(slice_assign), in_hbm(path), branches, in_hbm(stems.reshape(2, 2048, 256))))
    a2, c2 = matrices((slice_assign, path, branches, in_hbm(closing)))
    got = lax.all_to_all(send, ALL, 0, 0, tiled=True).reshape(8192, 128)
    out = after(in_hbm(got), a2, c2)
    out = out.reshape(2, 256, 2, 2, 128)
    return jnp.transpose(out, (0, 1, 3, 2, 4)).reshape(2, 256, 2, 256)


def solution(mesh):
    return jax.shard_map(
        per_device,
        mesh=mesh,
        in_specs=(P("cuts", None, "shard", None, None), P(), P(), P(), P()),
        out_specs=P(None, "shard", "cuts", None),
        check_vma=False,
    )
```

```python
import functools

import jax
import jax.numpy as jnp
from jax import lax
from jax.experimental import pallas as pl
from jax.experimental.pallas import tpu as pltpu
from jax.sharding import PartitionSpec as P

BF, F32 = jnp.bfloat16, jnp.float32
ALL = ("cuts", "shard")


def halves(x):
    high = x.astype(BF)
    return high, (x - high.astype(F32)).astype(BF)


def dot3(left, right):
    dot = functools.partial(jnp.dot, preferred_element_type=F32)
    rows = left.shape[0] // 2
    both = dot(left, right[0])
    return both[:rows] + (both[rows:] + dot(left[:rows], right[1]))


def stacked(x):
    return cat(halves(x), 0)


def put(pair, rows, cols, value):
    pair[0, rows, cols], pair[1, rows, cols] = halves(value)


def right_blocks(pair, part, value):
    one, two = slice(0, 256), slice(256, 512)
    if part == 0:
        put(pair, one, one, value)
        put(pair, two, two, value)
    else:
        put(pair, one, two, value)
        put(pair, two, one, -value)


def cat(pieces, axis):
    return jnp.concatenate(pieces, axis=axis)


def before_kernel(assign, path, branches, x, send, words, steps, xs, v, tmp, w1, w0, ys, word_sem, x_sem, v_sem, y_sem):
    words_in = [pltpu.make_async_copy(a, to, word_sem.at[i]) for i, (a, to) in enumerate(((assign, words), (path, steps)))]
    stem = [
        pltpu.make_async_copy(x.at[p, :, pl.ds(128 * h, 128)], xs.at[p, h], x_sem.at[p, h])
        for p in range(2)
        for h in range(2)
    ]
    for copy in words_in:
        copy.start()
    for copy in stem:
        copy.start()
    for copy in words_in:
        copy.wait()
    value = words[lax.axis_index("cuts")]
    turn_by = lax.rem(lax.axis_index("shard"), 8)
    weights = [pltpu.make_async_copy(branches.at[value, steps[i]], v.at[i], v_sem.at[i]) for i in range(2)]
    for copy in (weights[1], weights[0]):
        copy.start()

    def three(to, re, im):
        for k, matrix in enumerate((re, im - re, re + im)):
            to[k, 0], to[k, 1] = halves(matrix)

    def product(x, y, by):
        k1, k2, k3 = (dot3(stacked(a), (by[k, 0], by[k, 1])) for k, a in enumerate((x + y, x, y)))
        return k1 - k3, k1 + k2

    weights[1].wait()
    three(w1, v[1, 0], v[1, 1])
    weights[0].wait()
    sorted_parts = []
    for part in range(2):
        turned = v[0, part].T
        for h in range(2):
            tmp[h] = turned[:, 128 * h : 128 * h + 128]
        moved = [cat([tmp[h, pl.ds(b, 64, stride=4), :] for b in range(4)], 0) for h in range(2)]
        sorted_parts.append(cat(moved, 1).T)
    three(w0, *sorted_parts)
    for copy in stem:
        copy.wait()

    def along_k(m):
        return product(*(cat([xs[p, h, pl.ds(m, 256, stride=8), :] for h in range(2)], 1) for p in range(2)), w1)

    def write(m):
        where = pl.ds(32 * (m // 2), 32), slice(None), pl.ds(16 * (m % 2), 16)
        return pltpu.make_async_copy(ys.at[where], send.at[where], y_sem.at[m])

    later = [along_k(0), along_k(1)]
    upper = lax.broadcasted_iota(jnp.int32, (32, 8, 256), 1) < 4
    for m in range(8):
        c, parity = m // 2, m % 2
        z = later.pop(0)
        if m < 6:
            later.append(along_k(m + 2))
        re, im = (a.reshape(32, 8, 256) for a in product(z[0].T, z[1].T, w0))
        crossed = pltpu.roll(jnp.where(upper, im, re), 4, 1)
        for odd, pair in enumerate((jnp.where(upper, re, crossed), jnp.where(upper, crossed, im))):
            pair = pltpu.roll(pair, turn_by, 1)
            for bh in range(2):
                r = 16 * parity + 8 * bh
                ys[32 * c : 32 * c + 32, odd, r : r + 8, :] = pair[:, :, 128 * bh : 128 * bh + 128]
        write(m).start()
    for m in range(8):
        write(m).wait()


def matrices_kernel(assign, path, branches, closing, a2, c2, v, c, tmp, v_sem, c_sem):
    copies = [
        pltpu.make_async_copy(
            branches.at[assign[s], path[2], p, :, pl.ds(128 * h, 128)], v.at[s, p, h], v_sem.at[s, p, h]
        )
        for s in range(4)
        for p in range(2)
        for h in range(2)
    ]
    last = pltpu.make_async_copy(closing, c, c_sem)
    for copy in copies:
        copy.start()
    last.start()
    for copy in copies:
        copy.wait()
    for s in range(4):
        for p in range(2):
            moved = [cat([v[s, p, h, pl.ds(b, 64, stride=4), :] for b in range(4)], 0) for h in range(2)]
            at = 256 * p
            a2[s, at : at + 256, :], a2[s, 512 + at : 768 + at, :] = halves(cat(moved, 1).T)
    last.wait()
    for p in range(2):
        for h in range(2):
            tmp[h] = c[p, :, 128 * h : 128 * h + 128]
        moved = cat([cat([tmp[h, pl.ds(b, 64, stride=4), :] for b in range(4)], 0) for h in range(2)], 1)
        right_blocks(c2, p, moved)


def after_kernel(got, a2, c2, out, rs, os, r_sem, o_sem):
    def read(s):
        rows = pl.ds(2048 * s, 2048)
        return pltpu.make_async_copy(got.at[rows], rs.at[s, pl.ds(8, 2048)], r_sem.at[s])

    w = lax.broadcasted_iota(jnp.int32, (8, 128), 0)

    def row_of(s, block, j):
        rows = []
        for z in range(8):
            at = 256 * z + 8 * block + j + 8
            straight = rs[s, pl.ds(at, 8, stride=33), :]
            rows.append(jnp.where(w + j < 8, straight, rs[s, pl.ds(at - 8, 8, stride=33), :]) if j else straight)
        return cat(rows, 0)

    low_lane = lax.broadcasted_iota(jnp.int32, (64, 128), 1) < 64

    def sources(s, p, parity, bph):
        rows = []
        for bh in range(2):
            one, two = (row_of(s, 2 * parity + bh, 4 * p + 2 * bph + bpl) for bpl in range(2))
            crossed = pltpu.roll(jnp.where(low_lane, two, one), 64, 1)
            rows += [jnp.where(low_lane, one, crossed), jnp.where(low_lane, crossed, two)]
        return cat(rows, 0)

    def arrived(s):
        read(s).wait()
        re, im = (cat([sources(s, p, m, bph) for m in range(2) for bph in range(2)], 1) for p in range(2))
        return halves(re), halves(re + im), halves(im - re)

    for s in range(4):
        read(s).start()
        rs[s, 0:8] = rs[s, 2056:2064] = jnp.zeros((8, 128), F32)
    later, total = arrived(0), None
    for s in range(4):
        right = later
        if s < 3:
            later = arrived(s + 1)
        parts = [a2[s, 256 * i : 256 * i + 256] for i in range(4)]
        both = parts[0].astype(F32) + parts[2].astype(F32) + (parts[1].astype(F32) + parts[3].astype(F32))
        lefts = stacked(both), cat(parts[1::2], 0), cat(parts[::2], 0)
        terms = [dot3(*pair) for pair in zip(lefts, right, strict=True)]
        total = terms if total is None else [a + b for a, b in zip(total, terms, strict=True)]
    real, imaginary = total[0] - total[1], total[0] + total[2]
    left = cat([cat([real[:, cols], imaginary[:, cols]], 1) for cols in (slice(0, 256), slice(256, 512))], 0)
    left = stacked(left)
    writes = []
    for q in range(2):
        result = dot3(left, (c2[0, :, 256 * q : 256 * q + 256], c2[1, :, 256 * q : 256 * q + 256]))
        for parity in range(2):
            for h in range(2):
                value = result[256 * parity : 256 * parity + 256, 128 * h : 128 * h + 128]
                os[pl.ds(1024 * q + 2 * h + parity, 256, stride=4), :] = value
        rows = pl.ds(1024 * q, 1024)
        writes.append(pltpu.make_async_copy(os.at[rows], out.at[rows], o_sem.at[q]))
        writes[q].start()
    for copy in writes:
        copy.wait()


SMEM = pl.BlockSpec(memory_space=pltpu.SMEM)
HBM = pl.BlockSpec(memory_space=pltpu.HBM)
VMEM = pl.BlockSpec(memory_space=pltpu.VMEM)
DMA = pltpu.SemaphoreType.DMA


def kernel_call(kernel, in_specs, out_specs, shapes, operands, name, scratch, mib):
    return pl.pallas_call(
        kernel,
        in_specs=in_specs,
        out_specs=out_specs,
        out_shape=shapes,
        scratch_shapes=scratch,
        compiler_params=pltpu.CompilerParams(vmem_limit_bytes=mib * 2**20),
        name=name,
    )(*operands)


def shaped(*shape, dtype=F32):
    return jax.ShapeDtypeStruct(shape, dtype)


def before(operands):
    return kernel_call(
        before_kernel,
        [HBM] * 4,
        [HBM],
        [pltpu.HBM((128, 2, 32, 128), F32)],
        operands,
        "before",
        [
            pltpu.SMEM((6,), jnp.int32),
            pltpu.SMEM((3,), jnp.int32),
            pltpu.VMEM((2, 2, 2048, 128), F32),
            pltpu.VMEM((2, 2, 256, 256), F32),
            pltpu.VMEM((2, 256, 128), F32),
            pltpu.VMEM((3, 2, 256, 256), BF),
            pltpu.VMEM((3, 2, 256, 256), BF),
            pltpu.VMEM((128, 2, 32, 128), F32),
            DMA((2,)),
            DMA((2, 2)),
            DMA((2,)),
            DMA((8,)),
        ],
        32,
    )[0]


def matrices(operands):
    return kernel_call(
        matrices_kernel,
        [SMEM, SMEM, HBM, HBM],
        [VMEM, VMEM],
        [shaped(4, 1024, 256, dtype=BF), shaped(2, 512, 512, dtype=BF)],
        operands,
        "matrices",
        [
            pltpu.VMEM((4, 2, 2, 256, 128), F32),
            pltpu.VMEM((2, 256, 256), F32),
            pltpu.VMEM((2, 256, 128), F32),
            DMA((4, 2, 2)),
            DMA,
        ],
        24,
    )


def after(got, a2, c2):
    return kernel_call(
        after_kernel,
        [HBM, VMEM, VMEM],
        [HBM],
        [pltpu.HBM((2048, 128), F32)],
        (got, a2, c2),
        "after",
        [pltpu.VMEM((4, 2064, 128), F32), pltpu.VMEM((2048, 128), F32), DMA((4,)), DMA((2,))],
        28,
    )[0]


def in_hbm(a):
    return pltpu.with_memory_space_constraint(a, pltpu.HBM)


def per_device(stems, slice_branches, closing, path, slice_assign):
    branches = in_hbm(slice_branches)
    send = before((in_hbm(slice_assign), in_hbm(path), branches, in_hbm(stems.reshape(2, 2048, 256))))
    a2, c2 = matrices((slice_assign, path, branches, in_hbm(closing)))
    got = lax.all_to_all(send.reshape(256, 32, 128), ALL, 0, 0, tiled=True).reshape(8192, 128)
    out = after(in_hbm(got), a2, c2)
    out = out.reshape(2, 256, 2, 2, 128)
    return jnp.transpose(out, (0, 1, 3, 2, 4)).reshape(2, 256, 2, 256)


def solution(mesh):
    return jax.shard_map(
        per_device,
        mesh=mesh,
        in_specs=(P("cuts", None, "shard", None, None), P(), P(), P(), P()),
        out_specs=P(None, "shard", "cuts", None),
        check_vma=False,
    )
```

```python
import functools

import jax
import jax.numpy as jnp
from jax import lax
from jax.experimental import pallas as pl
from jax.experimental.pallas import tpu as pltpu
from jax.sharding import PartitionSpec as P

BF, F32 = jnp.bfloat16, jnp.float32
ALL = ("cuts", "shard")


def halves(x):
    high = x.astype(BF)
    return high, (x - high.astype(F32)).astype(BF)


def dot3(left, right):
    dot = functools.partial(jnp.dot, preferred_element_type=F32)
    rows = left.shape[0] // 2
    both = dot(left, right[0])
    return both[:rows] + (both[rows:] + dot(left[:rows], right[1]))


def stacked(x):
    return cat(halves(x), 0)


def cat(pieces, axis):
    return jnp.concatenate(pieces, axis=axis)


def three(to, re, im):
    for k, matrix in enumerate((re, im - re, re + im)):
        to[k, 0], to[k, 1] = halves(matrix)


def product(x, y, by):
    k1, k2, k3 = (dot3(stacked(a), (by[k, 0], by[k, 1])) for k, a in enumerate((x + y, x, y)))
    return k1 - k3, k1 + k2


def before_kernel(assign, path, branches, x, send, words, steps, xs, v, tmp, w1, w0, ys, word_sem, x_sem, v_sem, y_sem):
    words_in = [pltpu.make_async_copy(a, to, word_sem.at[i]) for i, (a, to) in enumerate(((assign, words), (path, steps)))]
    stem = [
        pltpu.make_async_copy(x.at[p, :, pl.ds(128 * h, 128)], xs.at[p, h], x_sem.at[p, h])
        for p in range(2)
        for h in range(2)
    ]
    for copy in words_in:
        copy.start()
    for copy in stem:
        copy.start()
    for copy in words_in:
        copy.wait()
    value = words[lax.axis_index("cuts")]
    turn_by = lax.rem(lax.axis_index("shard"), 8)
    weights = [pltpu.make_async_copy(branches.at[value, steps[i]], v.at[i], v_sem.at[i]) for i in range(2)]
    for copy in (weights[1], weights[0]):
        copy.start()

    weights[1].wait()
    three(w1, v[1, 0], v[1, 1])
    for copy in stem:
        copy.wait()

    def along_k(m):
        return product(*(cat([xs[p, h, pl.ds(m, 256, stride=8), :] for h in range(2)], 1) for p in range(2)), w1)

    def write(m):
        where = pl.ds(32 * (m // 2), 32), slice(None), pl.ds(16 * (m % 2), 16)
        return pltpu.make_async_copy(ys.at[where], send.at[where], y_sem.at[m])

    later = [along_k(0)]
    weights[0].wait()
    sorted_parts = []
    for part in range(2):
        turned = v[0, part].T
        for h in range(2):
            tmp[h] = turned[:, 128 * h : 128 * h + 128]
        moved = [cat([tmp[h, pl.ds(b, 64, stride=4), :] for b in range(4)], 0) for h in range(2)]
        sorted_parts.append(cat(moved, 1).T)
    three(w0, *sorted_parts)
    later.append(along_k(1))
    upper = lax.broadcasted_iota(jnp.int32, (32, 8, 256), 1) < 4
    for m in range(8):
        c, parity = m // 2, m % 2
        z = later.pop(0)
        if m < 6:
            later.append(along_k(m + 2))
        re, im = (a.reshape(32, 8, 256) for a in product(z[0].T, z[1].T, w0))
        crossed = pltpu.roll(jnp.where(upper, im, re), 4, 1)
        for odd, pair in enumerate((jnp.where(upper, re, crossed), jnp.where(upper, crossed, im))):
            pair = pltpu.roll(pair, turn_by, 1)
            for bh in range(2):
                r = 16 * parity + 8 * bh
                ys[32 * c : 32 * c + 32, odd, r : r + 8, :] = pair[:, :, 128 * bh : 128 * bh + 128]
        write(m).start()
    for m in range(8):
        write(m).wait()


def matrices_kernel(assign, path, branches, closing, a2, c2, v, c, tmp, v_sem, c_sem):
    copies = [
        pltpu.make_async_copy(
            branches.at[assign[s], path[2], p, :, pl.ds(128 * h, 128)], v.at[s, p, h], v_sem.at[s, p, h]
        )
        for s in range(4)
        for p in range(2)
        for h in range(2)
    ]
    last = pltpu.make_async_copy(closing, c, c_sem)
    for copy in copies:
        copy.start()
    last.start()
    for copy in copies:
        copy.wait()
    for s in range(4):
        for p in range(2):
            moved = [cat([v[s, p, h, pl.ds(b, 64, stride=4), :] for b in range(4)], 0) for h in range(2)]
            at = 256 * p
            a2[s, at : at + 256, :], a2[s, 512 + at : 768 + at, :] = halves(cat(moved, 1).T)
    last.wait()
    parts = []
    for p in range(2):
        for h in range(2):
            tmp[h] = c[p, :, 128 * h : 128 * h + 128]
        parts.append(cat([cat([tmp[h, pl.ds(b, 64, stride=4), :] for b in range(4)], 0) for h in range(2)], 1))
    three(c2, *parts)


def after_kernel(got, a2, c2, out, rs, os, r_sem, o_sem):
    def read(s):
        rows = pl.ds(2048 * s, 2048)
        return pltpu.make_async_copy(got.at[rows], rs.at[s, pl.ds(8, 2048)], r_sem.at[s])

    w = lax.broadcasted_iota(jnp.int32, (8, 128), 0)

    def row_of(s, block, j):
        rows = []
        for z in range(8):
            at = 256 * z + 8 * block + j + 8
            straight = rs[s, pl.ds(at, 8, stride=33), :]
            rows.append(jnp.where(w + j < 8, straight, rs[s, pl.ds(at - 8, 8, stride=33), :]) if j else straight)
        return cat(rows, 0)

    low_lane = lax.broadcasted_iota(jnp.int32, (64, 128), 1) < 64

    def sources(s, p, parity, bph):
        rows = []
        for bh in range(2):
            one, two = (row_of(s, 2 * parity + bh, 4 * p + 2 * bph + bpl) for bpl in range(2))
            crossed = pltpu.roll(jnp.where(low_lane, two, one), 64, 1)
            rows += [jnp.where(low_lane, one, crossed), jnp.where(low_lane, crossed, two)]
        return cat(rows, 0)

    def arrived(s):
        read(s).wait()
        re, im = (cat([sources(s, p, m, bph) for m in range(2) for bph in range(2)], 1) for p in range(2))
        return halves(re), halves(re + im), halves(im - re)

    for s in range(4):
        read(s).start()
        rs[s, 0:8] = rs[s, 2056:2064] = jnp.zeros((8, 128), F32)
    later, total = arrived(0), None
    for s in range(4):
        right = later
        if s < 3:
            later = arrived(s + 1)
        parts = [a2[s, 256 * i : 256 * i + 256] for i in range(4)]
        both = parts[0].astype(F32) + parts[2].astype(F32) + (parts[1].astype(F32) + parts[3].astype(F32))
        lefts = stacked(both), cat(parts[1::2], 0), cat(parts[::2], 0)
        terms = [dot3(*pair) for pair in zip(lefts, right, strict=True)]
        total = terms if total is None else [a + b for a, b in zip(total, terms, strict=True)]
    real, imaginary = total[0] - total[1], total[0] + total[2]
    sides = (cat([a[:, :256], a[:, 256:]], 0) for a in (real, imaginary))
    writes = []
    for q, result in enumerate(product(*sides, c2)):
        for parity in range(2):
            for h in range(2):
                value = result[256 * parity : 256 * parity + 256, 128 * h : 128 * h + 128]
                os[pl.ds(1024 * q + 2 * h + parity, 256, stride=4), :] = value
        rows = pl.ds(1024 * q, 1024)
        writes.append(pltpu.make_async_copy(os.at[rows], out.at[rows], o_sem.at[q]))
        writes[q].start()
    for copy in writes:
        copy.wait()


SMEM = pl.BlockSpec(memory_space=pltpu.SMEM)
HBM = pl.BlockSpec(memory_space=pltpu.HBM)
VMEM = pl.BlockSpec(memory_space=pltpu.VMEM)
DMA = pltpu.SemaphoreType.DMA


def kernel_call(kernel, in_specs, out_specs, shapes, operands, name, scratch, mib):
    return pl.pallas_call(
        kernel,
        in_specs=in_specs,
        out_specs=out_specs,
        out_shape=shapes,
        scratch_shapes=scratch,
        compiler_params=pltpu.CompilerParams(vmem_limit_bytes=mib * 2**20),
        name=name,
    )(*operands)


def shaped(*shape, dtype=F32):
    return jax.ShapeDtypeStruct(shape, dtype)


def before(operands):
    return kernel_call(
        before_kernel,
        [HBM] * 4,
        [HBM],
        [pltpu.HBM((128, 2, 32, 128), F32)],
        operands,
        "before",
        [
            pltpu.SMEM((6,), jnp.int32),
            pltpu.SMEM((3,), jnp.int32),
            pltpu.VMEM((2, 2, 2048, 128), F32),
            pltpu.VMEM((2, 2, 256, 256), F32),
            pltpu.VMEM((2, 256, 128), F32),
            pltpu.VMEM((3, 2, 256, 256), BF),
            pltpu.VMEM((3, 2, 256, 256), BF),
            pltpu.VMEM((128, 2, 32, 128), F32),
            DMA((2,)),
            DMA((2, 2)),
            DMA((2,)),
            DMA((8,)),
        ],
        32,
    )[0]


def matrices(operands):
    return kernel_call(
        matrices_kernel,
        [SMEM, SMEM, HBM, HBM],
        [VMEM, VMEM],
        [shaped(4, 1024, 256, dtype=BF), shaped(3, 2, 256, 256, dtype=BF)],
        operands,
        "matrices",
        [
            pltpu.VMEM((4, 2, 2, 256, 128), F32),
            pltpu.VMEM((2, 256, 256), F32),
            pltpu.VMEM((2, 256, 128), F32),
            DMA((4, 2, 2)),
            DMA,
        ],
        24,
    )


def after(got, a2, c2):
    return kernel_call(
        after_kernel,
        [HBM, VMEM, VMEM],
        [HBM],
        [pltpu.HBM((2048, 128), F32)],
        (got, a2, c2),
        "after",
        [pltpu.VMEM((4, 2064, 128), F32), pltpu.VMEM((2048, 128), F32), DMA((4,)), DMA((2,))],
        28,
    )[0]


def in_hbm(a):
    return pltpu.with_memory_space_constraint(a, pltpu.HBM)


def per_device(stems, slice_branches, closing, path, slice_assign):
    branches = in_hbm(slice_branches)
    send = before((in_hbm(slice_assign), in_hbm(path), branches, in_hbm(stems.reshape(2, 2048, 256))))
    a2, c2 = matrices((slice_assign, path, branches, in_hbm(closing)))
    got = lax.all_to_all(send.reshape(256, 32, 128), ALL, 0, 0, tiled=True).reshape(8192, 128)
    out = after(in_hbm(got), a2, c2)
    out = out.reshape(2, 256, 2, 2, 128)
    return jnp.transpose(out, (0, 1, 3, 2, 4)).reshape(2, 256, 2, 256)


def solution(mesh):
    return jax.shard_map(
        per_device,
        mesh=mesh,
        in_specs=(P("cuts", None, "shard", None, None), P(), P(), P(), P()),
        out_specs=P(None, "shard", "cuts", None),
        check_vma=False,
    )
```
